32 devices in a mesh: leaf: 2 (over core), row: 4 (over z), col: 4 (over y, x).
Axes of the slice: x: 2, y: 2, z: 4, core: 2. Of those that a mesh axis runs over, the one named last changes fastest.
Arguments:
- front: float32 [2, 16, 4, 128, 16, 4, 128], P('leaf', None, 'row', None, None, 'col'), as said below
- parent: float32 [8, 2, 4, 128, 16, 4, 128], P(None, 'leaf', 'row', None, None, 'col'), may hold values from -0.2 to 0.2
- tile_map: int32 [2, 56], replicated, may hold values from 0 to 63, as said below
- col_shift: int32 [16], replicated, may hold values from 0 to 3
Outputs:
- factored: float32 [2, 16, 4, 128, 16, 4, 128], P('leaf', None, 'row', None, None, 'col')
- new_parent: float32 [8, 2, 4, 128, 16, 4, 128], P(None, 'leaf', 'row', None, None, 'col')
The draws below stay inside these ranges and needn't reach their ends.
Inputs may be any that keep to these rules, and one draw needn't show every extreme that they name: For each leaf the 8192 x 8192 matrix read from front is symmetric positive definite. Entry [l, e] names the parent tile joined by tile 8 + e of child l; no row repeats a value. The parent tile q = tile_map[l, e] has (q mod 4 + col_shift[q // 4]) mod 4 equal to (8 + e) mod 4. Among the tiles of one child whose indices are equal mod 4, at most 4 have parent tiles equal mod 8.
All inputs are finite; a program needn't handle non-finite values.
Results may differ from the reference program's by a relative error of at most 0.0001.
Values sent between devices are 32-bit elements; how exact they have to be, the bound alone decides.
A program may use at most 192 MiB of HBM per device.

```python
import jax
import jax.numpy as jnp
from jax import lax

F = 8192
TILE = 128
PB = 512
PANELS = 2
NPIV = 1024
PRS = 8
PCS = 16
N_LEAF = 2
N_ROW = 4
N_COL = 4


def draw_front(key, part):
    subkeys = jax.random.split(jax.random.fold_in(key, 7), 3)
    factor_width = 4 * PB
    factors = jax.random.normal(subkeys[0], (N_LEAF, F, factor_width), jnp.float32)
    scales = jnp.exp(jax.random.uniform(subkeys[1], (N_LEAF, F), jnp.float32, jnp.log(0.5), jnp.log(2.0)))
    shifts = jnp.exp(jax.random.uniform(subkeys[2], (N_LEAF, F), jnp.float32, jnp.log(0.5), jnp.log(2.0)))
    scaled = factors * (scales / jnp.sqrt(jnp.float32(factor_width)))[:, :, None]
    gram_part = jnp.einsum('lip,ljp->lij', scaled, scaled, precision=lax.Precision.HIGHEST)
    diagonal_ids = jnp.arange(F)
    matrix = gram_part.at[:, diagonal_ids, diagonal_ids].add(shifts)
    return matrix.reshape(N_LEAF, F // (TILE * N_ROW), N_ROW, TILE, F // (TILE * N_COL), N_COL, TILE)


def assembly_maps(key):
    tile_count = F // TILE
    pivot_tiles = NPIV // TILE
    column_slots = tile_count // N_COL
    repeats = (column_slots + N_ROW - 1) // N_ROW
    shift_pool = jnp.arange(repeats * N_ROW, dtype=jnp.int32) % N_ROW
    shuffled = jax.random.permutation(jax.random.fold_in(key, 31), shift_pool)
    col_shift = shuffled[:column_slots].astype(jnp.int32)
    tile_maps = []
    for leaf_index in range(N_LEAF):
        score_key = jax.random.fold_in(key, 41 + leaf_index)
        scores = jax.random.randint(score_key, (N_COL, column_slots), 0, 1 << 20, dtype=jnp.int32) * column_slots + jnp.arange(column_slots, dtype=jnp.int32)[None, :]
        ordering = jnp.argsort(scores, axis=1, stable=True).astype(jnp.int32)
        child_tiles = jnp.arange(pivot_tiles, tile_count, dtype=jnp.int32)
        column_owner = child_tiles % N_COL
        column_slot = child_tiles // N_COL
        parent_slot = ordering[column_owner, column_slot]
        tile_maps.append(N_COL * parent_slot + (column_owner - col_shift[parent_slot]) % N_COL)
    return (jnp.stack(tile_maps).astype(jnp.int32), col_shift)


def draw_tile_map(key, part):
    return assembly_maps(key)[0]


def draw_col_shift(key, part):
    return assembly_maps(key)[1]


def block_levels(key, dims, cuts, low, high):
    def one(axis_at, shards_of):
        heights = jax.random.uniform(jax.random.fold_in(jax.random.fold_in(key, 6), axis_at), (shards_of,), jnp.float32, low / len(cuts), high / len(cuts))
        return jnp.repeat(jnp.exp(heights), dims[axis_at] // shards_of).reshape((-1,) + (1,) * (len(dims) - axis_at - 1))

    level = one(*cuts[0])
    for cut in cuts[1:]:
        level = level * one(*cut)
    return level


def centred(stream_key, shape, deviation, reach, cuts=(), kind=jnp.bfloat16):
    values = deviation * jax.random.normal(stream_key, shape, jnp.float32)
    if cuts:
        values = values * block_levels(stream_key, shape, cuts, -0.22, 0.18)
    return jnp.clip(values, -reach, reach).astype(kind)


def setup_inputs(seed: int = 0) -> dict:
    key_list = jax.random.split(jax.random.key(seed), 5)
    front = draw_front(jax.random.fold_in(key_list[4], 71), 0)
    parent = centred(key_list[1], (PRS, N_LEAF, N_ROW, TILE, PCS, N_COL, TILE), 0.03, 0.2, ((1, 2), (2, 4), (5, 4)), jnp.float32)
    tile_map = draw_tile_map(jax.random.fold_in(key_list[4], 71), 0)
    col_shift = draw_col_shift(jax.random.fold_in(key_list[4], 71), 0)
    return {"front": front, "parent": parent, "tile_map": tile_map, "col_shift": col_shift}


def factor_leaf(matrix):
    for panel_index in range(PANELS):
        panel_start = panel_index * PB
        panel_end = panel_start + PB
        lower_factor = jnp.linalg.cholesky(matrix[panel_start:panel_end, panel_start:panel_end])
        below_panel = lax.linalg.triangular_solve(lower_factor, matrix[panel_end:, panel_start:panel_end], left_side=False, lower=True, transpose_a=True)
        product = jnp.dot(below_panel.astype(jnp.float32), below_panel.T.astype(jnp.float32), precision=lax.Precision.HIGHEST, preferred_element_type=jnp.float32)
        matrix = matrix.at[panel_end:, panel_end:].add(-product)
        matrix = matrix.at[panel_start:panel_end, panel_start:panel_end].set(lower_factor)
        matrix = matrix.at[panel_end:, panel_start:panel_end].set(below_panel)
    row_ids = jnp.arange(F, dtype=jnp.int32)[:, None]
    col_ids = jnp.arange(F, dtype=jnp.int32)[None, :]
    kept_mask = (col_ids < NPIV) & (row_ids >= col_ids) | (col_ids >= NPIV) & (row_ids >= NPIV)
    return jnp.where(kept_mask, matrix, jnp.zeros_like(matrix))

def reference(front, parent, tile_map, col_shift):
    tile_count = F // TILE
    contrib_tiles = tile_count - NPIV // TILE
    full_fronts = front.reshape(N_LEAF, F, F)
    assembled = jnp.zeros((tile_count, TILE, tile_count, TILE), jnp.float32)
    factored_list = []
    for leaf_index in range(N_LEAF):
        factored_leaf = factor_leaf(full_fronts[leaf_index])
        factored_list.append(factored_leaf)
        contribution = factored_leaf[NPIV:, NPIV:].reshape(contrib_tiles, TILE, contrib_tiles, TILE).transpose(0, 2, 1, 3)
        targets = tile_map[leaf_index].astype(jnp.int32)
        assembled = assembled.at[targets[:, None], :, targets[None, :], :].add(contribution)
    factored = jnp.stack(factored_list).reshape(front.shape)
    slot_of_tile = (jnp.arange(tile_count, dtype=jnp.int32) // N_COL).astype(jnp.int32)
    owners = (jnp.arange(tile_count, dtype=jnp.int32) % N_COL).astype(jnp.int32)
    source = (slot_of_tile * N_COL + (owners - col_shift[slot_of_tile]) % N_COL).astype(jnp.int32)
    stored = jnp.take(assembled, source, axis=2)
    new_parent = parent + stored.reshape(parent.shape)
    return (factored, new_parent)
```

```python
import jax
import jax.numpy as jnp
from jax import lax
from jax.experimental import pallas as pl
from jax.experimental.pallas import tpu as pltpu
from jax.sharding import PartitionSpec as P

TILE = 128
PB = 512
PANELS = 2
NPIV = 1024


HIGHEST = lax.Precision.HIGHEST
HIGH = lax.Precision.HIGH


def spread(value, axis, source):
    kept = jnp.where(lax.axis_index(axis) == source, value, 0).astype(value.dtype)
    return lax.psum(kept, axis)


def update_slots(working, next_rows, column_factor, slot_low, slot_high):
    product = jnp.einsum(
        "atp,bsp->atbs",
        next_rows,
        column_factor,
        precision=HIGHEST,
        preferred_element_type=jnp.float32,
    )
    return working.at[:, :, slot_low:slot_high, :].add(-product)


def per_device(front, parent, tile_map, col_shift):
    leaf_count = lax.axis_size("leaf")
    row_count = lax.axis_size("row")
    col_count = lax.axis_size("col")
    leaf_index = lax.axis_index("leaf")
    row_index = lax.axis_index("row")
    col_index = lax.axis_index("col")
    local_front = front[0, :, 0, :, :, 0, :]
    row_slots = local_front.shape[0]
    col_slots = local_front.shape[2]
    panel_tiles = PB // TILE
    pivot_tiles = NPIV // TILE
    row_tiles = jnp.arange(row_slots, dtype=jnp.int32) * row_count + row_index
    col_tiles = jnp.arange(col_slots, dtype=jnp.int32) * col_count + col_index

    def fetch_panel(working, panel_index):
        pieces = []
        for offset in range(panel_tiles):
            column = panel_index * panel_tiles + offset
            column_tile = working[:, :, column // col_count, :]
            pieces.append(spread(column_tile, "col", column % col_count))
        return jnp.concatenate(pieces, axis=2)

    def write_factor(working, factor, panel_index):
        first_column = panel_index * panel_tiles
        slot_values = sorted(
            set([(first_column + offset) // col_count for offset in range(panel_tiles)])
        )
        for slot_index in slot_values:
            current = working[:, :, slot_index, :]
            for offset in range(panel_tiles):
                column = first_column + offset
                if column // col_count == slot_index:
                    current = jnp.where(
                        col_index == column % col_count,
                        factor[:, :, offset * TILE : (offset + 1) * TILE],
                        current,
                    )
            working = working.at[:, :, slot_index, :].set(current)
        return working

    working = local_front
    panel_block = fetch_panel(working, 0)
    for panel_index in range(PANELS):
        first_tile = panel_index * panel_tiles
        factor_slot_index = first_tile // row_count
        start_row = first_tile % row_count
        gathered = lax.all_gather(panel_block[factor_slot_index], "row", axis=0, tiled=True)
        diagonal_block = gathered[start_row * TILE : (start_row + panel_tiles) * TILE]
        lower_factor = jnp.linalg.cholesky(diagonal_block)
        factor_flattened = panel_block.reshape(row_slots * TILE, PB)
        solved = lax.linalg.triangular_solve(
            lower_factor, factor_flattened, left_side=False, lower=True, transpose_a=True
        )
        solved = solved.reshape(row_slots, TILE, PB)
        offset_tile = jnp.clip(row_index - start_row, 0, panel_tiles - 1)
        diagonal_rows = lax.dynamic_slice_in_dim(lower_factor, offset_tile * TILE, TILE, 0)
        in_panel = (row_tiles >= first_tile) & (row_tiles < first_tile + panel_tiles)
        factor_factor = jnp.where(in_panel[:, None, None], diagonal_rows[None], solved)
        factor_factor = jnp.where((row_tiles >= first_tile)[:, None, None], factor_factor, 0.0)
        next_rows = jnp.where(
            (row_tiles >= first_tile + panel_tiles)[:, None, None], factor_factor, 0.0
        )
        group_size = col_count // row_count
        owner_rows = spread(next_rows, "row", col_index % row_count)
        grouped = owner_rows.reshape(col_slots, group_size, TILE, PB)
        column_factor = lax.dynamic_index_in_dim(grouped, col_index // row_count, 1, keepdims=False)
        column_factor = jnp.where(
            (col_tiles >= first_tile + panel_tiles)[:, None, None], column_factor, 0.0
        )
        factor, next_rows, column_factor = (factor_factor, next_rows, column_factor)
        working = update_slots(working, next_rows, column_factor, 0, col_slots)
        upcoming = (
            fetch_panel(working, panel_index + 1) if panel_index + 1 < PANELS else panel_block
        )
        working = write_factor(working, factor, panel_index)
        panel_block = upcoming
    upper_part = (row_tiles < pivot_tiles)[:, None, None, None] & (col_tiles >= pivot_tiles)[
        None, None, :, None
    ]
    working = jnp.where(upper_part, 0.0, working)
    factored = working.reshape(front.shape)
    contribution = jnp.where((col_tiles >= pivot_tiles)[None, None, :, None], working, 0.0)
    contrib_count = tile_map.shape[1]
    entry_ids = jnp.arange(contrib_count, dtype=jnp.int32)
    own_map = lax.dynamic_index_in_dim(tile_map, leaf_index, 0, keepdims=False)
    row_match = (row_tiles - pivot_tiles)[:, None] == entry_ids[None, :]
    row_targets = jnp.sum(jnp.where(row_match, own_map[None, :], 0), axis=1)
    row_valid = row_tiles >= pivot_tiles
    owner_count = leaf_count * row_count
    destination = row_targets % owner_count
    parent_row_slot = row_targets // owner_count
    slot_ids = jnp.arange(row_slots, dtype=jnp.int32)
    same_before = (
        (destination[None, :] == destination[:, None])
        & row_valid[None, :]
        & (slot_ids[None, :] < slot_ids[:, None])
    )
    rank_in_dest = jnp.sum(same_before.astype(jnp.int32), axis=1)
    capacity = (col_slots + row_count - 1) // row_count
    owner_ids = jnp.arange(owner_count, dtype=jnp.int32)
    capacity_ids = jnp.arange(capacity, dtype=jnp.int32)
    selection = (
        row_valid[None, None, :]
        & (destination[None, None, :] == owner_ids[:, None, None])
        & (rank_in_dest[None, None, :] == capacity_ids[None, :, None])
    )
    flattened = contribution.reshape(row_slots, -1)
    send_buffer = jnp.einsum(
        "oka,ax->okx",
        selection.astype(jnp.float32),
        flattened,
        precision=HIGHEST,
        preferred_element_type=jnp.float32,
    )
    chosen_slot = jnp.sum(jnp.where(selection, parent_row_slot[None, None, :], 0), axis=2)
    send_slots = jnp.where(jnp.any(selection, axis=2), chosen_slot, -1)
    received, received_slots = (
        lax.all_to_all(send_buffer, ("leaf", "row"), split_axis=0, concat_axis=0, tiled=True),
        lax.all_to_all(send_slots, ("leaf", "row"), split_axis=0, concat_axis=0, tiled=True),
    )
    received = received.reshape(leaf_count, row_count, capacity, -1)
    received_slots = received_slots.reshape(leaf_count, row_count, capacity)
    parent_local = parent[:, 0, 0, :, :, 0, :]
    parent_rows = parent_local.shape[0]
    parent_cols = parent_local.shape[2]
    row_place = (
        received_slots[None] == jnp.arange(parent_rows, dtype=jnp.int32)[:, None, None, None]
    ).astype(jnp.float32)
    by_leaf = jnp.einsum(
        "slrk,lrkx->slx", row_place, received, precision=HIGHEST, preferred_element_type=jnp.float32
    )
    by_leaf = by_leaf.reshape(parent_rows, leaf_count, TILE, col_slots, TILE)
    col_match = (col_tiles - pivot_tiles)[:, None] == entry_ids[None, :]
    col_targets = jnp.sum(jnp.where(col_match[None], tile_map[:, None, :], 0), axis=2)
    col_valid = col_tiles >= pivot_tiles
    parent_slot_ids = jnp.arange(parent_cols, dtype=jnp.int32)
    col_place = (
        col_valid[None, None, :]
        & (col_targets[:, None, :] // col_count == parent_slot_ids[None, :, None])
    ).astype(jnp.float32)
    assembled = jnp.einsum(
        "sltbv,lub->stuv", by_leaf, col_place, precision=HIGHEST, preferred_element_type=jnp.float32
    )
    new_parent = (parent_local + assembled).reshape(parent.shape)
    return (factored, new_parent)


def factor_kernel(a_ref, lower_ref, inverse_ref, work, upper, small):
    order = a_ref.shape[0]
    blocks = order // TILE
    tiles = TILE // 8
    work[...] = a_ref[...]
    lower_ref[...] = jnp.zeros_like(lower_ref)
    inverse_ref[...] = jnp.zeros_like(inverse_ref)
    lanes = lax.broadcasted_iota(jnp.int32, (8, TILE), 1)
    subs = lax.broadcasted_iota(jnp.int32, (8, TILE), 0)
    sub_column = lax.broadcasted_iota(jnp.int32, (8, 1), 0)

    def dot(a, b, dims):
        return lax.dot_general(
            a, b, (dims, ((), ())), precision=HIGHEST, preferred_element_type=jnp.float32
        )

    def step(block, carry):
        start = pl.multiple_of(block * TILE, TILE)
        a = [work[pl.ds(start + 8 * i, 8), pl.ds(start, TILE)] for i in range(tiles)]
        w = [jnp.where(lanes == subs + 8 * i, 1.0, 0.0).astype(jnp.float32) for i in range(tiles)]
        for k in range(TILE):
            home, sub = k // 8, k % 8
            row_a = a[home][sub : sub + 1, :]
            row_w = w[home][sub : sub + 1, :]
            scale = lax.rsqrt(jnp.broadcast_to(row_a[:, k : k + 1], (1, TILE)))
            row_a = row_a * scale
            row_w = row_w * scale
            for i in range(home, tiles):
                column = jnp.broadcast_to(a[i][:, k : k + 1], (8, TILE)) * scale
                if i == home:
                    column = jnp.where(subs > sub, column, 0.0)
                a[i] = a[i] - column * row_a
                w[i] = w[i] - column * row_w
            a[home] = jnp.where(subs == sub, row_a, a[home])
            w[home] = jnp.where(subs == sub, row_w, w[home])
        for i in range(tiles):
            upper[8 * i : 8 * i + 8, :] = jnp.where(lanes >= subs + 8 * i, a[i], 0.0)
            small[8 * i : 8 * i + 8, :] = w[i]
        for b in range(blocks):

            @pl.when(block == b)
            def _():
                low, high = b * TILE, (b + 1) * TILE
                inv = small[...]
                lower_ref[low:high, low:high] = upper[...].T
                inverse_ref[low:high, low:high] = inv
                if b:
                    inverse_ref[low:high, :low] = dot(inv, inverse_ref[low:high, :low], ((1,), (0,)))
                if b + 1 < blocks:
                    below = dot(work[high:, low:high], inv, ((1,), (1,)))
                    lower_ref[high:, low:high] = below
                    work[high:, high:] -= dot(below, below, ((1,), (1,)))
                    inverse_ref[high:, :high] -= dot(below, inverse_ref[low:high, :high], ((1,), (0,)))

        return carry

    lax.fori_loop(0, blocks, step, 0)


def factor_leading(matrix):
    order = matrix.shape[0]
    shape = jax.ShapeDtypeStruct((order, order), jnp.float32)
    return pl.pallas_call(
        factor_kernel,
        out_shape=(shape, shape),
        in_specs=[pl.BlockSpec(memory_space=pltpu.VMEM)],
        out_specs=(pl.BlockSpec(memory_space=pltpu.VMEM),) * 2,
        scratch_shapes=[
            pltpu.VMEM((order, order), jnp.float32),
            pltpu.VMEM((TILE, TILE), jnp.float32),
            pltpu.VMEM((TILE, TILE), jnp.float32),
        ],
        compiler_params=pltpu.CompilerParams(vmem_limit_bytes=56 * 1024 * 1024),
        cost_estimate=pl.CostEstimate(
            flops=4 * order**3, bytes_accessed=12 * order**2, transcendentals=0
        ),
        name="factor_leading",
    )(matrix)


def place_kernel(row_ids, col_ids, source_ref, out_ref):
    row_id = row_ids[pl.program_id(0)]
    for k in range(out_ref.shape[1] // TILE):
        col_id = col_ids[k]
        start = pl.multiple_of(jnp.maximum(col_id, 0) * TILE, TILE)
        tile = source_ref[:, pl.ds(start, TILE)]
        kept = (row_id >= 0) & (col_id >= 0)
        out_ref[:, k * TILE : (k + 1) * TILE] = jnp.where(kept, tile, 0.0)


def place(source, row_ids, col_ids):
    rows, cols = row_ids.shape[0], col_ids.shape[0]
    width = source.shape[1]
    return pl.pallas_call(
        place_kernel,
        grid_spec=pltpu.PrefetchScalarGridSpec(
            num_scalar_prefetch=2,
            grid=(rows,),
            in_specs=[pl.BlockSpec((TILE, width), lambda g, r, c: (jnp.maximum(r[g], 0), 0))],
            out_specs=pl.BlockSpec((TILE, cols * TILE), lambda g, r, c: (g, 0)),
        ),
        out_shape=jax.ShapeDtypeStruct((rows * TILE, cols * TILE), jnp.float32),
        compiler_params=pltpu.CompilerParams(vmem_limit_bytes=32 * 1024 * 1024),
        cost_estimate=pl.CostEstimate(
            flops=0, bytes_accessed=4 * rows * TILE * (width + cols * TILE), transcendentals=0
        ),
        name="place",
    )(row_ids, col_ids, source)


def add_kernel(row_ids, half, parent_ref, own_ref, other_ref, out_ref):
    width = own_ref.shape[1]
    own_cols = pl.ds(pl.multiple_of(half[0] * width, TILE), width)
    other_cols = pl.ds(pl.multiple_of((1 - half[0]) * width, TILE), width)
    out_ref[:, own_cols] = parent_ref[:, own_cols] + own_ref[...]
    out_ref[:, other_cols] = parent_ref[:, other_cols] + other_ref[...]


def add_rows(parent, own, other, row_ids, half):
    rows, width = row_ids.shape[0], own.shape[1]
    whole = pl.BlockSpec((TILE, 2 * width), lambda g, r, h: (g, 0))
    return pl.pallas_call(
        add_kernel,
        grid_spec=pltpu.PrefetchScalarGridSpec(
            num_scalar_prefetch=2,
            grid=(rows,),
            in_specs=[
                whole,
                pl.BlockSpec((TILE, width), lambda g, r, h: (r[g], 0)),
                pl.BlockSpec((TILE, width), lambda g, r, h: (g, 0)),
            ],
            out_specs=whole,
        ),
        out_shape=jax.ShapeDtypeStruct(parent.shape, jnp.float32),
        compiler_params=pltpu.CompilerParams(vmem_limit_bytes=32 * 1024 * 1024),
        name="add_rows",
    )(row_ids, half, parent, own, other)


def per_device_square(front, parent, tile_map, col_shift):
    side = lax.axis_size("row")
    leaf_index = lax.axis_index("leaf")
    row_index = lax.axis_index("row")
    col_index = lax.axis_index("col")
    x = front[0, :, 0, :, :, 0, :]
    row_slots, _, col_slots, _ = x.shape
    pivot_tiles = NPIV // TILE
    first = pivot_tiles // side
    rest_rows, rest_cols = row_slots - first, col_slots - first

    leading = lax.all_gather(x[:first, :, :first, :], ("row", "col"))
    leading = leading.reshape(side, side, first, TILE, first, TILE)
    leading = leading.transpose(2, 0, 3, 4, 1, 5).reshape(NPIV, NPIV)
    panel_rows = lax.all_gather(x[first:, :, :first, :], "col")
    panel_rows = panel_rows.transpose(1, 2, 3, 0, 4).reshape(rest_rows * TILE, NPIV)
    panel_cols = lax.all_gather(x[:first, :, first:, :], "row")
    panel_cols = panel_cols.transpose(1, 0, 2, 3, 4).reshape(NPIV, rest_cols * TILE)

    lower, inverse = factor_leading(leading)
    row_factor = lax.dot_general(
        panel_rows, inverse, (((1,), (1,)), ((), ())), precision=HIGH,
        preferred_element_type=jnp.float32,
    )
    col_factor = lax.dot_general(
        inverse, panel_cols, (((1,), (0,)), ((), ())), precision=HIGH,
        preferred_element_type=jnp.float32,
    )
    rest = x[first:, :, first:, :].reshape(rest_rows * TILE, rest_cols * TILE)
    rest = rest - lax.dot_general(
        row_factor, col_factor, (((1,), (0,)), ((), ())), precision=HIGH,
        preferred_element_type=jnp.float32,
    )

    slots = jnp.arange(col_slots, dtype=jnp.int32)
    own_map = lax.dynamic_index_in_dim(tile_map, leaf_index, 0, keepdims=False)
    own_slots = (own_map // side).reshape(-1, side)
    row_target = lax.dynamic_index_in_dim(own_slots, row_index, 1, keepdims=False)
    col_target = lax.dynamic_index_in_dim(own_slots, col_index, 1, keepdims=False)

    def source_of(target):
        match = target[None, :] == slots[:, None]
        ids = jnp.arange(target.shape[0], dtype=jnp.int32)
        return jnp.sum(jnp.where(match, ids[None, :] + 1, 0), axis=1) - 1

    before = (col_shift[None, :] < col_shift[:, None]) | (
        (col_shift[None, :] == col_shift[:, None]) & (slots[None, :] < slots[:, None])
    )
    rank = jnp.sum(before.astype(jnp.int32), axis=1)
    in_order = (rank[None, :] == slots[:, None]).astype(jnp.int32)
    row_source = jnp.sum(in_order * source_of(row_target)[None, :], axis=1)
    sorted_shift = jnp.sum(in_order * col_shift[None, :], axis=1)
    col_source = source_of(col_target).reshape(2, -1)
    half = col_slots // 2

    swap = [(0, 1), (1, 0)]
    away = place(rest, row_source, col_source[1 - leaf_index])
    came = lax.ppermute(away, "leaf", swap)
    stays = place(rest, row_source, col_source[leaf_index])
    summed = stays + came

    share = col_slots // side

    def by_groups(value):
        pieces = [value[: share * TILE]]
        for shift in range(1, side):
            piece = value[shift * share * TILE : (shift + 1) * share * TILE]
            perm = [(r, (r - shift) % side) for r in range(side)]
            pieces.append(lax.ppermute(piece, "row", perm))
        return jnp.concatenate(pieces, axis=0)

    def by_gather(value):
        everything = lax.all_gather(value, "row").reshape(side, col_slots, TILE, half * TILE)
        pieces = []
        for slot in range(col_slots):
            origin = (row_index + sorted_shift[slot]) % side
            pieces.append(lax.dynamic_index_in_dim(everything[:, slot], origin, 0, keepdims=False))
        return jnp.concatenate(pieces, axis=0)

    even = jnp.all(sorted_shift == slots // share)
    rotated = lax.cond(even, by_groups, by_gather, summed)

    position = rank.reshape(-1, 2)
    across = place(
        rotated,
        lax.dynamic_index_in_dim(position, 1 - leaf_index, 1, keepdims=False),
        jnp.arange(half, dtype=jnp.int32),
    )
    other = lax.ppermute(across, "leaf", swap)
    parent_local = parent[:, 0, 0, :, :, 0, :].reshape(-1, col_slots * TILE)
    new_parent = add_rows(
        parent_local,
        rotated,
        other,
        lax.dynamic_index_in_dim(position, leaf_index, 1, keepdims=False),
        leaf_index.astype(jnp.int32)[None],
    ).reshape(parent.shape)

    own_rows = lax.dynamic_index_in_dim(
        lower.reshape(first, side, TILE, first, side, TILE), row_index, 1, keepdims=False
    )
    own_corner = lax.dynamic_index_in_dim(own_rows, col_index, 3, keepdims=False)
    own_below = lax.dynamic_index_in_dim(
        row_factor.reshape(rest_rows, TILE, first, side, TILE), col_index, 3, keepdims=False
    )
    top = jnp.concatenate(
        [own_corner, jnp.zeros((first, TILE, rest_cols, TILE), jnp.float32)], axis=2
    )
    bottom = jnp.concatenate(
        [own_below, rest.reshape(rest_rows, TILE, rest_cols, TILE)], axis=2
    )
    factored = jnp.concatenate([top, bottom], axis=0).reshape(front.shape)
    return (factored, new_parent)


def solution(mesh):
    sizes = dict(mesh.shape)
    square = (
        sizes["leaf"] == 2 and sizes["row"] == sizes["col"] and NPIV % (TILE * sizes["row"]) == 0
    )
    return jax.shard_map(
        per_device_square if square else per_device,
        mesh=mesh,
        in_specs=(
            P("leaf", None, "row", None, None, "col", None),
            P(None, "leaf", "row", None, None, "col", None),
            P(),
            P(),
        ),
        out_specs=(
            P("leaf", None, "row", None, None, "col", None),
            P(None, "leaf", "row", None, None, "col", None),
        ),
        check_vma=False,
    )
```

```python
import jax
import jax.numpy as jnp
from jax import lax
from jax.experimental import pallas as pl
from jax.experimental.pallas import tpu as pltpu
from jax.sharding import PartitionSpec as P

TILE = 128
PB = 512
PANELS = 2
NPIV = 1024


HIGHEST = lax.Precision.HIGHEST
HIGH = lax.Precision.HIGH


def spread(value, axis, source):
    kept = jnp.where(lax.axis_index(axis) == source, value, 0).astype(value.dtype)
    return lax.psum(kept, axis)


def update_slots(working, next_rows, column_factor, slot_low, slot_high):
    product = jnp.einsum(
        "atp,bsp->atbs",
        next_rows,
        column_factor,
        precision=HIGHEST,
        preferred_element_type=jnp.float32,
    )
    return working.at[:, :, slot_low:slot_high, :].add(-product)


def per_device(front, parent, tile_map, col_shift):
    leaf_count = lax.axis_size("leaf")
    row_count = lax.axis_size("row")
    col_count = lax.axis_size("col")
    leaf_index = lax.axis_index("leaf")
    row_index = lax.axis_index("row")
    col_index = lax.axis_index("col")
    local_front = front[0, :, 0, :, :, 0, :]
    row_slots = local_front.shape[0]
    col_slots = local_front.shape[2]
    panel_tiles = PB // TILE
    pivot_tiles = NPIV // TILE
    row_tiles = jnp.arange(row_slots, dtype=jnp.int32) * row_count + row_index
    col_tiles = jnp.arange(col_slots, dtype=jnp.int32) * col_count + col_index

    def fetch_panel(working, panel_index):
        pieces = []
        for offset in range(panel_tiles):
            column = panel_index * panel_tiles + offset
            column_tile = working[:, :, column // col_count, :]
            pieces.append(spread(column_tile, "col", column % col_count))
        return jnp.concatenate(pieces, axis=2)

    def write_factor(working, factor, panel_index):
        first_column = panel_index * panel_tiles
        slot_values = sorted(
            set([(first_column + offset) // col_count for offset in range(panel_tiles)])
        )
        for slot_index in slot_values:
            current = working[:, :, slot_index, :]
            for offset in range(panel_tiles):
                column = first_column + offset
                if column // col_count == slot_index:
                    current = jnp.where(
                        col_index == column % col_count,
                        factor[:, :, offset * TILE : (offset + 1) * TILE],
                        current,
                    )
            working = working.at[:, :, slot_index, :].set(current)
        return working

    working = local_front
    panel_block = fetch_panel(working, 0)
    for panel_index in range(PANELS):
        first_tile = panel_index * panel_tiles
        factor_slot_index = first_tile // row_count
        start_row = first_tile % row_count
        gathered = lax.all_gather(panel_block[factor_slot_index], "row", axis=0, tiled=True)
        diagonal_block = gathered[start_row * TILE : (start_row + panel_tiles) * TILE]
        lower_factor = jnp.linalg.cholesky(diagonal_block)
        factor_flattened = panel_block.reshape(row_slots * TILE, PB)
        solved = lax.linalg.triangular_solve(
            lower_factor, factor_flattened, left_side=False, lower=True, transpose_a=True
        )
        solved = solved.reshape(row_slots, TILE, PB)
        offset_tile = jnp.clip(row_index - start_row, 0, panel_tiles - 1)
        diagonal_rows = lax.dynamic_slice_in_dim(lower_factor, offset_tile * TILE, TILE, 0)
        in_panel = (row_tiles >= first_tile) & (row_tiles < first_tile + panel_tiles)
        factor_factor = jnp.where(in_panel[:, None, None], diagonal_rows[None], solved)
        factor_factor = jnp.where((row_tiles >= first_tile)[:, None, None], factor_factor, 0.0)
        next_rows = jnp.where(
            (row_tiles >= first_tile + panel_tiles)[:, None, None], factor_factor, 0.0
        )
        group_size = col_count // row_count
        owner_rows = spread(next_rows, "row", col_index % row_count)
        grouped = owner_rows.reshape(col_slots, group_size, TILE, PB)
        column_factor = lax.dynamic_index_in_dim(grouped, col_index // row_count, 1, keepdims=False)
        column_factor = jnp.where(
            (col_tiles >= first_tile + panel_tiles)[:, None, None], column_factor, 0.0
        )
        factor, next_rows, column_factor = (factor_factor, next_rows, column_factor)
        working = update_slots(working, next_rows, column_factor, 0, col_slots)
        upcoming = (
            fetch_panel(working, panel_index + 1) if panel_index + 1 < PANELS else panel_block
        )
        working = write_factor(working, factor, panel_index)
        panel_block = upcoming
    upper_part = (row_tiles < pivot_tiles)[:, None, None, None] & (col_tiles >= pivot_tiles)[
        None, None, :, None
    ]
    working = jnp.where(upper_part, 0.0, working)
    factored = working.reshape(front.shape)
    contribution = jnp.where((col_tiles >= pivot_tiles)[None, None, :, None], working, 0.0)
    contrib_count = tile_map.shape[1]
    entry_ids = jnp.arange(contrib_count, dtype=jnp.int32)
    own_map = lax.dynamic_index_in_dim(tile_map, leaf_index, 0, keepdims=False)
    row_match = (row_tiles - pivot_tiles)[:, None] == entry_ids[None, :]
    row_targets = jnp.sum(jnp.where(row_match, own_map[None, :], 0), axis=1)
    row_valid = row_tiles >= pivot_tiles
    owner_count = leaf_count * row_count
    destination = row_targets % owner_count
    parent_row_slot = row_targets // owner_count
    slot_ids = jnp.arange(row_slots, dtype=jnp.int32)
    same_before = (
        (destination[None, :] == destination[:, None])
        & row_valid[None, :]
        & (slot_ids[None, :] < slot_ids[:, None])
    )
    rank_in_dest = jnp.sum(same_before.astype(jnp.int32), axis=1)
    capacity = (col_slots + row_count - 1) // row_count
    owner_ids = jnp.arange(owner_count, dtype=jnp.int32)
    capacity_ids = jnp.arange(capacity, dtype=jnp.int32)
    selection = (
        row_valid[None, None, :]
        & (destination[None, None, :] == owner_ids[:, None, None])
        & (rank_in_dest[None, None, :] == capacity_ids[None, :, None])
    )
    flattened = contribution.reshape(row_slots, -1)
    send_buffer = jnp.einsum(
        "oka,ax->okx",
        selection.astype(jnp.float32),
        flattened,
        precision=HIGHEST,
        preferred_element_type=jnp.float32,
    )
    chosen_slot = jnp.sum(jnp.where(selection, parent_row_slot[None, None, :], 0), axis=2)
    send_slots = jnp.where(jnp.any(selection, axis=2), chosen_slot, -1)
    received, received_slots = (
        lax.all_to_all(send_buffer, ("leaf", "row"), split_axis=0, concat_axis=0, tiled=True),
        lax.all_to_all(send_slots, ("leaf", "row"), split_axis=0, concat_axis=0, tiled=True),
    )
    received = received.reshape(leaf_count, row_count, capacity, -1)
    received_slots = received_slots.reshape(leaf_count, row_count, capacity)
    parent_local = parent[:, 0, 0, :, :, 0, :]
    parent_rows = parent_local.shape[0]
    parent_cols = parent_local.shape[2]
    row_place = (
        received_slots[None] == jnp.arange(parent_rows, dtype=jnp.int32)[:, None, None, None]
    ).astype(jnp.float32)
    by_leaf = jnp.einsum(
        "slrk,lrkx->slx", row_place, received, precision=HIGHEST, preferred_element_type=jnp.float32
    )
    by_leaf = by_leaf.reshape(parent_rows, leaf_count, TILE, col_slots, TILE)
    col_match = (col_tiles - pivot_tiles)[:, None] == entry_ids[None, :]
    col_targets = jnp.sum(jnp.where(col_match[None], tile_map[:, None, :], 0), axis=2)
    col_valid = col_tiles >= pivot_tiles
    parent_slot_ids = jnp.arange(parent_cols, dtype=jnp.int32)
    col_place = (
        col_valid[None, None, :]
        & (col_targets[:, None, :] // col_count == parent_slot_ids[None, :, None])
    ).astype(jnp.float32)
    assembled = jnp.einsum(
        "sltbv,lub->stuv", by_leaf, col_place, precision=HIGHEST, preferred_element_type=jnp.float32
    )
    new_parent = (parent_local + assembled).reshape(parent.shape)
    return (factored, new_parent)


def factor_kernel(a_ref, lower_ref, inverse_ref, work, upper, small):
    order = a_ref.shape[0]
    blocks = order // TILE
    tiles = TILE // 8
    work[...] = a_ref[...]
    lower_ref[...] = jnp.zeros_like(lower_ref)
    inverse_ref[...] = jnp.zeros_like(inverse_ref)
    lanes = lax.broadcasted_iota(jnp.int32, (8, TILE), 1)
    subs = lax.broadcasted_iota(jnp.int32, (8, TILE), 0)
    sub_column = lax.broadcasted_iota(jnp.int32, (8, 1), 0)

    def dot(a, b, dims):
        return lax.dot_general(
            a, b, (dims, ((), ())), precision=HIGHEST, preferred_element_type=jnp.float32
        )

    def step(block, carry):
        start = pl.multiple_of(block * TILE, TILE)
        a = [work[pl.ds(start + 8 * i, 8), pl.ds(start, TILE)] for i in range(tiles)]
        w = [jnp.where(lanes == subs + 8 * i, 1.0, 0.0).astype(jnp.float32) for i in range(tiles)]
        for k in range(TILE):
            home, sub = k // 8, k % 8
            row_a = a[home][sub : sub + 1, :]
            row_w = w[home][sub : sub + 1, :]
            scale = lax.rsqrt(jnp.broadcast_to(row_a[:, k : k + 1], (1, TILE)))
            row_a = row_a * scale
            row_w = row_w * scale
            for i in range(home, tiles):
                column = jnp.broadcast_to(a[i][:, k : k + 1], (8, TILE)) * scale
                if i == home:
                    column = jnp.where(subs > sub, column, 0.0)
                a[i] = a[i] - column * row_a
                w[i] = w[i] - column * row_w
            a[home] = jnp.where(subs == sub, row_a, a[home])
            w[home] = jnp.where(subs == sub, row_w, w[home])
        for i in range(tiles):
            upper[8 * i : 8 * i + 8, :] = jnp.where(lanes >= subs + 8 * i, a[i], 0.0)
            small[8 * i : 8 * i + 8, :] = w[i]
        for b in range(blocks):

            @pl.when(block == b)
            def _():
                low, high = b * TILE, (b + 1) * TILE
                inv = small[...]
                lower_ref[low:high, low:high] = upper[...].T
                inverse_ref[low:high, low:high] = inv
                if b:
                    inverse_ref[low:high, :low] = dot(inv, inverse_ref[low:high, :low], ((1,), (0,)))
                if b + 1 < blocks:
                    below = dot(work[high:, low:high], inv, ((1,), (1,)))
                    lower_ref[high:, low:high] = below
                    work[high:, high:] -= dot(below, below, ((1,), (1,)))
                    inverse_ref[high:, :high] -= dot(below, inverse_ref[low:high, :high], ((1,), (0,)))

        return carry

    lax.fori_loop(0, blocks, step, 0)


def factor_leading(matrix):
    order = matrix.shape[0]
    shape = jax.ShapeDtypeStruct((order, order), jnp.float32)
    return pl.pallas_call(
        factor_kernel,
        out_shape=(shape, shape),
        in_specs=[pl.BlockSpec(memory_space=pltpu.VMEM)],
        out_specs=(pl.BlockSpec(memory_space=pltpu.VMEM),) * 2,
        scratch_shapes=[
            pltpu.VMEM((order, order), jnp.float32),
            pltpu.VMEM((TILE, TILE), jnp.float32),
            pltpu.VMEM((TILE, TILE), jnp.float32),
        ],
        compiler_params=pltpu.CompilerParams(vmem_limit_bytes=56 * 1024 * 1024),
        cost_estimate=pl.CostEstimate(
            flops=4 * order**3, bytes_accessed=12 * order**2, transcendentals=0
        ),
        name="factor_leading",
    )(matrix)


def place_kernel(row_ids, col_ids, source_ref, out_ref):
    row_id = row_ids[pl.program_id(0)]
    for k in range(out_ref.shape[1] // TILE):
        col_id = col_ids[k]
        start = pl.multiple_of(jnp.maximum(col_id, 0) * TILE, TILE)
        tile = source_ref[:, pl.ds(start, TILE)]
        kept = (row_id >= 0) & (col_id >= 0)
        out_ref[:, k * TILE : (k + 1) * TILE] = jnp.where(kept, tile, 0.0)


def place(source, row_ids, col_ids):
    rows, cols = row_ids.shape[0], col_ids.shape[0]
    width = source.shape[1]
    return pl.pallas_call(
        place_kernel,
        grid_spec=pltpu.PrefetchScalarGridSpec(
            num_scalar_prefetch=2,
            grid=(rows,),
            in_specs=[pl.BlockSpec((TILE, width), lambda g, r, c: (jnp.maximum(r[g], 0), 0))],
            out_specs=pl.BlockSpec((TILE, cols * TILE), lambda g, r, c: (g, 0)),
        ),
        out_shape=jax.ShapeDtypeStruct((rows * TILE, cols * TILE), jnp.float32),
        compiler_params=pltpu.CompilerParams(vmem_limit_bytes=32 * 1024 * 1024),
        cost_estimate=pl.CostEstimate(
            flops=0, bytes_accessed=4 * rows * TILE * (width + cols * TILE), transcendentals=0
        ),
        name="place",
    )(row_ids, col_ids, source)


def add_kernel(row_ids, half, parent_ref, own_ref, other_ref, out_ref):
    width = own_ref.shape[1]
    own_cols = pl.ds(pl.multiple_of(half[0] * width, TILE), width)
    other_cols = pl.ds(pl.multiple_of((1 - half[0]) * width, TILE), width)
    out_ref[:, own_cols] = parent_ref[:, own_cols] + own_ref[...]
    out_ref[:, other_cols] = parent_ref[:, other_cols] + other_ref[...]


def add_rows(parent, own, other, row_ids, half):
    rows, width = row_ids.shape[0], own.shape[1]
    whole = pl.BlockSpec((TILE, 2 * width), lambda g, r, h: (g, 0))
    return pl.pallas_call(
        add_kernel,
        grid_spec=pltpu.PrefetchScalarGridSpec(
            num_scalar_prefetch=2,
            grid=(rows,),
            in_specs=[
                whole,
                pl.BlockSpec((TILE, width), lambda g, r, h: (r[g], 0)),
                pl.BlockSpec((TILE, width), lambda g, r, h: (g, 0)),
            ],
            out_specs=whole,
        ),
        out_shape=jax.ShapeDtypeStruct(parent.shape, jnp.float32),
        compiler_params=pltpu.CompilerParams(vmem_limit_bytes=32 * 1024 * 1024),
        name="add_rows",
    )(row_ids, half, parent, own, other)


def per_device_square(front, parent, tile_map, col_shift):
    side = lax.axis_size("row")
    leaf_index = lax.axis_index("leaf")
    row_index = lax.axis_index("row")
    col_index = lax.axis_index("col")
    x = front[0, :, 0, :, :, 0, :]
    row_slots, _, col_slots, _ = x.shape
    pivot_tiles = NPIV // TILE
    first = pivot_tiles // side
    rest_rows, rest_cols = row_slots - first, col_slots - first

    leading = lax.all_gather(x[:first, :, :first, :], ("row", "col"))
    leading = leading.reshape(side, side, first, TILE, first, TILE)
    leading = leading.transpose(2, 0, 3, 4, 1, 5).reshape(NPIV, NPIV)
    panel_rows = x[first:, :, :first, :].reshape(rest_rows * TILE, first * TILE)
    panel_rows = lax.all_gather(panel_rows, "col", axis=1, tiled=True)
    own_cols = x[:first, :, first:, :].reshape(first * TILE, rest_cols * TILE)
    pieces = [own_cols]
    for shift in range(1, side):
        perm = [(r, (r - shift) % side) for r in range(side)]
        pieces.append(lax.ppermute(own_cols, "row", perm))
    panel_cols = jnp.concatenate(pieces, axis=0)

    lower, inverse = factor_leading(leading)
    by_col = [
        inverse[:, (b * side + c) * TILE : (b * side + c + 1) * TILE]
        for c in range(side)
        for b in range(first)
    ]
    by_row = [
        lax.dynamic_slice_in_dim(inverse, (a * side + (row_index + shift) % side) * TILE, TILE, 1)
        for shift in range(side)
        for a in range(first)
    ]
    row_factor = lax.dot_general(
        panel_rows, jnp.concatenate(by_col, axis=1), (((1,), (1,)), ((), ())), precision=HIGH,
        preferred_element_type=jnp.float32,
    )
    col_factor = lax.dot_general(
        jnp.concatenate(by_row, axis=1), panel_cols, (((1,), (0,)), ((), ())), precision=HIGH,
        preferred_element_type=jnp.float32,
    )
    rest = x[first:, :, first:, :].reshape(rest_rows * TILE, rest_cols * TILE)
    rest = rest - lax.dot_general(
        row_factor, col_factor, (((1,), (0,)), ((), ())), precision=HIGH,
        preferred_element_type=jnp.float32,
    )

    slots = jnp.arange(col_slots, dtype=jnp.int32)
    own_map = lax.dynamic_index_in_dim(tile_map, leaf_index, 0, keepdims=False)
    own_slots = (own_map // side).reshape(-1, side)
    row_target = lax.dynamic_index_in_dim(own_slots, row_index, 1, keepdims=False)
    col_target = lax.dynamic_index_in_dim(own_slots, col_index, 1, keepdims=False)

    def source_of(target):
        match = target[None, :] == slots[:, None]
        ids = jnp.arange(target.shape[0], dtype=jnp.int32)
        return jnp.sum(jnp.where(match, ids[None, :] + 1, 0), axis=1) - 1

    before = (col_shift[None, :] < col_shift[:, None]) | (
        (col_shift[None, :] == col_shift[:, None]) & (slots[None, :] < slots[:, None])
    )
    rank = jnp.sum(before.astype(jnp.int32), axis=1)
    in_order = (rank[None, :] == slots[:, None]).astype(jnp.int32)
    row_source = jnp.sum(in_order * source_of(row_target)[None, :], axis=1)
    sorted_shift = jnp.sum(in_order * col_shift[None, :], axis=1)
    col_source = source_of(col_target).reshape(2, -1)
    half = col_slots // 2

    swap = [(0, 1), (1, 0)]
    away = place(rest, row_source, col_source[1 - leaf_index])
    came = lax.ppermute(away, "leaf", swap)
    stays = place(rest, row_source, col_source[leaf_index])
    summed = stays + came

    share = col_slots // side

    def by_groups(value):
        pieces = [value[: share * TILE]]
        for shift in range(1, side):
            piece = value[shift * share * TILE : (shift + 1) * share * TILE]
            perm = [(r, (r - shift) % side) for r in range(side)]
            pieces.append(lax.ppermute(piece, "row", perm))
        return jnp.concatenate(pieces, axis=0)

    def by_gather(value):
        everything = lax.all_gather(value, "row").reshape(side, col_slots, TILE, half * TILE)
        pieces = []
        for slot in range(col_slots):
            origin = (row_index + sorted_shift[slot]) % side
            pieces.append(lax.dynamic_index_in_dim(everything[:, slot], origin, 0, keepdims=False))
        return jnp.concatenate(pieces, axis=0)

    own_rows = lax.dynamic_index_in_dim(
        lower.reshape(first, side, TILE, first, side, TILE), row_index, 1, keepdims=False
    )
    own_corner = lax.dynamic_index_in_dim(own_rows, col_index, 3, keepdims=False)
    own_below = lax.dynamic_index_in_dim(
        row_factor.reshape(rest_rows, TILE, first, side, TILE), col_index, 3, keepdims=False
    )
    top = jnp.concatenate(
        [own_corner, jnp.zeros((first, TILE, rest_cols, TILE), jnp.float32)], axis=2
    )
    bottom = jnp.concatenate(
        [own_below, rest.reshape(rest_rows, TILE, rest_cols, TILE)], axis=2
    )
    factored = jnp.concatenate([top, bottom], axis=0).reshape(front.shape)
    parent_local = parent[:, 0, 0, :, :, 0, :].reshape(-1, col_slots * TILE)
    grouped, factored, parent_local = lax.optimization_barrier(
        (by_groups(summed), factored, parent_local)
    )

    even = jnp.all(sorted_shift == slots // share)
    rotated = lax.cond(
        even, lambda grouped, value: grouped, lambda grouped, value: by_gather(value),
        grouped, summed,
    )

    position = rank.reshape(-1, 2)
    across = place(
        rotated,
        lax.dynamic_index_in_dim(position, 1 - leaf_index, 1, keepdims=False),
        jnp.arange(half, dtype=jnp.int32),
    )
    other = lax.ppermute(across, "leaf", swap)
    new_parent = add_rows(
        parent_local,
        rotated,
        other,
        lax.dynamic_index_in_dim(position, leaf_index, 1, keepdims=False),
        leaf_index.astype(jnp.int32)[None],
    ).reshape(parent.shape)

    return (factored, new_parent)


def solution(mesh):
    sizes = dict(mesh.shape)
    square = (
        sizes["leaf"] == 2 and sizes["row"] == sizes["col"] and NPIV % (TILE * sizes["row"]) == 0
    )
    return jax.shard_map(
        per_device_square if square else per_device,
        mesh=mesh,
        in_specs=(
            P("leaf", None, "row", None, None, "col", None),
            P(None, "leaf", "row", None, None, "col", None),
            P(),
            P(),
        ),
        out_specs=(
            P("leaf", None, "row", None, None, "col", None),
            P(None, "leaf", "row", None, None, "col", None),
        ),
        check_vma=False,
    )
```
